32 devices in a mesh: section: 16 (over z, y, x), grp: 2 (over core).
Axes of the slice: x: 2, y: 2, z: 4, core: 2. Of those that a mesh axis runs over, the one named last changes fastest.
Arguments:
- planes: bfloat16 [4, 64, 64, 2048], P(None, 'section', None, 'grp'), may hold values from -6 to 6
- w_reduce: bfloat16 [3, 2048, 2048], P(None, None, 'grp'), may hold values from -0.125 to 0.125
- w_group: bfloat16 [3, 9, 32, 2048], P(None, None, None, 'grp'), may hold values from -0.375 to 0.375
- w_expand: bfloat16 [3, 2048, 2048], P(None, None, 'grp'), may hold values from -0.125 to 0.125
- gains: float32 [3, 3, 2048], P(None, None, 'grp'), may hold values from 0.25 to 1.75
- biases: float32 [3, 3, 2048], P(None, None, 'grp'), may hold values from -1.5 to 1.5
Outputs:
- feats: bfloat16 [4, 64, 64, 2048], P(None, 'section', None, 'grp')
The draws below stay inside these ranges and needn't reach their ends.
All inputs are finite; a program needn't handle non-finite values.
Results may differ from the reference program's by a relative error of at most 0.014.
Values may be sent and summed in bfloat16 or wider, within the bound.
A program may use at most 192 MiB of HBM per device.

```python
import jax
import jax.numpy as jnp
from jax import lax

C = 2048
GW = 32
SIDE = 64
TILES = 4
BLOCKS = 3


def shard_levels(rng, shape, split, low, largest):
    gain, own = 1.0, jax.random.fold_in(rng, 6)
    for axis_at, parts in split:
        steps = jnp.exp(jax.random.uniform(jax.random.fold_in(own, axis_at), (parts,), jnp.float32, low / len(split), largest / len(split)))
        gain = gain * jnp.repeat(steps, shape[axis_at] // parts).reshape([-1 if axis == axis_at else 1 for axis in range(len(shape))])
    return gain


def scatter_about(own_key, dims, spread, limit, shards=(), kind=jnp.bfloat16):
    values = spread * jax.random.normal(own_key, dims, jnp.float32)
    if shards:
        values = values * shard_levels(own_key, dims, shards, -0.22, 0.18)
    return jnp.clip(values, -limit, limit).astype(kind)


def setup_inputs(seed: int = 0) -> dict:
    streams_of = jax.random.split(jax.random.key(seed), 7)
    return {
        "planes": scatter_about(streams_of[0], (TILES, SIDE, SIDE, C), 1.0, 6.0, ((1, 16), (3, 2))),
        "w_reduce": scatter_about(streams_of[1], (BLOCKS, C, C), C ** -0.5, 0.125, ((2, 2),)),
        "w_group": scatter_about(streams_of[2], (BLOCKS, 9, GW, C), (9 * GW) ** -0.5, 0.375, ((3, 2),)),
        "w_expand": scatter_about(streams_of[3], (BLOCKS, C, C), C ** -0.5, 0.125, ((2, 2),)),
        "gains": jnp.clip(1.0 + 0.15 * jax.random.normal(streams_of[4], (BLOCKS, 3, C), jnp.float32), 0.25, 1.75),
        "biases": scatter_about(streams_of[5], (BLOCKS, 3, C), 0.3, 1.5, ((2, 2),), jnp.float32),
    }


def run_block(planes, w_reduce, kernel, w_expand, gains, biases):
    channels = planes.shape[3]
    stream = planes.reshape(-1, channels)
    first = jnp.dot(stream, w_reduce, preferred_element_type=jnp.float32)
    hidden = jnp.maximum(gains[0] * first + biases[0], 0.0).astype(jnp.bfloat16)
    group_width = kernel.shape[1]
    filters = kernel.astype(jnp.float32).reshape(3, 3, group_width, channels)
    spatial = lax.conv_general_dilated(
        hidden.reshape(planes.shape).astype(jnp.float32), filters, (1, 1), "SAME",
        dimension_numbers=("NHWC", "HWIO", "NHWC"),
        feature_group_count=channels // group_width,
        precision=lax.Precision.HIGHEST).reshape(-1, channels)
    middle = jnp.maximum(gains[1] * spatial + biases[1], 0.0).astype(jnp.bfloat16)
    second = jnp.dot(middle, w_expand, preferred_element_type=jnp.float32)
    result = jnp.maximum(gains[2] * second + biases[2] + stream.astype(jnp.float32), 0.0)
    return result.astype(jnp.bfloat16).reshape(planes.shape)


def reference(planes, w_reduce, w_group, w_expand, gains, biases):
    current = planes
    for block in range(BLOCKS):
        current = run_block(current, w_reduce[block], w_group[block], w_expand[block], gains[block], biases[block])
    return current
```

```python
import functools

import jax
import jax.numpy as jnp
from jax import lax
from jax.experimental import pallas as pl
from jax.experimental.pallas import tpu as pltpu
from jax.sharding import PartitionSpec as P


def extended(cells, sides, width):
    for axis, dim in sides:
        count = lax.axis_size(axis)
        ends = count - 1
        head = lax.slice_in_dim(cells, 0, width, axis=dim)
        tail = lax.slice_in_dim(cells, cells.shape[dim] - width, cells.shape[dim], axis=dim)
        cells = jnp.concatenate(
            [
                lax.ppermute(tail, axis, [(i, (i + 1) % count) for i in range(ends)]),
                cells,
                lax.ppermute(head, axis, [((i + 1) % count, i) for i in range(ends)]),
            ],
            axis=dim,
        )
    return cells


def group_matrix(kernel):
    tap_count, group_width, channels = kernel.shape
    tiled = jnp.tile(kernel, (1, channels // group_width, 1))
    row_group = lax.broadcasted_iota(jnp.int32, (channels, channels), 0) // group_width
    col_group = lax.broadcasted_iota(jnp.int32, (channels, channels), 1) // group_width
    masked = jnp.where((row_group == col_group)[None], tiled, jnp.zeros_like(tiled))
    return masked.reshape(tap_count * channels, channels)


def contract(weight, piece):
    return jnp.dot(piece, weight, preferred_element_type=jnp.float32)


def gather_reduce(flat, weight):
    return contract(weight, lax.all_gather(flat, "grp", axis=1, tiled=True))


def gather_expand(flat, weight):
    return contract(weight, lax.all_gather(flat, "grp", axis=1, tiled=True))


def run_block(planes, w_reduce, kernel, w_expand, gains, biases):
    tiles, rows, breadth, channels = planes.shape
    dense_group = group_matrix(kernel)
    first = gather_reduce(planes.reshape(-1, channels), w_reduce)
    hidden = jnp.maximum(gains[0] * first + biases[0], 0.0).astype(jnp.bfloat16)
    hidden = extended(hidden.reshape(planes.shape), (("section", 1),), 1)
    padded = jnp.pad(hidden, ((0, 0), (0, 0), (1, 1), (0, 0)))
    shifted = [
        padded[:, row_shift : row_shift + rows, col_shift : col_shift + breadth, :]
        for row_shift in range(3)
        for col_shift in range(3)
    ]
    taps = jnp.concatenate(shifted, axis=-1).reshape(tiles * rows * breadth, 9 * channels)
    spatial = jnp.dot(taps, dense_group, preferred_element_type=jnp.float32)
    middle = jnp.maximum(gains[1] * spatial + biases[1], 0.0).astype(jnp.bfloat16)
    second = gather_expand(middle, w_expand)
    stream = planes.reshape(-1, channels).astype(jnp.float32)
    result = jnp.maximum(gains[2] * second + biases[2] + stream, 0.0)
    return result.astype(jnp.bfloat16).reshape(planes.shape)


def local(planes, w_reduce, w_group, w_expand, gains, biases):
    current = planes
    for block in range(w_reduce.shape[0]):
        current = run_block(
            current, w_reduce[block], w_group[block], w_expand[block], gains[block], biases[block]
        )
    return current


BLOCK = 256
MESH = pl.DeviceIdType.MESH


def fused_kernel(
    count, planes, w_reduce, w_group, w_expand, gains, biases, out,
    own, peer, mid, mid_peer, hid, halo, w_one, w_two, dense, taps,
    local_sem, weight_sem, swap_send, swap_recv, lift_send, lift_recv,
    cur_send, cur_recv, mid_send, mid_recv, halo_send, halo_recv, out_send, out_recv,
):
    blocks, depth, channels = w_reduce.shape[0], w_reduce.shape[1], planes.shape[2]
    part = planes.shape[1]
    whole = 2 * part
    breadth = halo.shape[3]
    pieces = channels // BLOCK
    units = own.shape[0]
    width = w_group.shape[1] // 9
    section, core = lax.axis_index("section"), lax.axis_index("grp")
    side = lax.rem(section, 2)
    twin = section + 1 - 2 * side
    above, below = section >= 2, section < count - 2
    other_core = {"grp": 1 - core}
    own_rows = pl.ds(pl.multiple_of(core * channels, channels), channels)
    peer_rows = pl.ds(pl.multiple_of((1 - core) * channels, channels), channels)
    mine = pl.ds(pl.multiple_of(side * part, part), part)
    theirs = pl.ds(pl.multiple_of((1 - side) * part, part), part)

    def remote(src, dst, send, recv, to):
        return pltpu.make_async_remote_copy(
            src_ref=src, dst_ref=dst, send_sem=send, recv_sem=recv, device_id=to, device_id_type=MESH)

    def swap(unit):
        return remote(planes.at[units * (1 - side) + unit], own.at[unit, mine],
                      swap_send.at[unit], swap_recv.at[unit], {"section": twin})

    def lift_first(unit):
        return remote(planes.at[units * side + unit], peer.at[unit, mine],
                      lift_send.at[0, unit], lift_recv.at[0, unit], other_core)

    def lift_second(unit):
        return remote(own.at[unit, theirs], peer.at[unit, theirs],
                      lift_send.at[1, unit], lift_recv.at[1, unit], other_core)

    def columns(piece):
        return pl.ds(pl.multiple_of(piece * BLOCK, BLOCK), BLOCK)

    def cur_copy(block, unit, piece):
        return remote(own.at[unit, :, columns(piece)], peer.at[unit, :, columns(piece)],
                      cur_send.at[block, unit, piece], cur_recv.at[block, unit, piece], other_core)

    def mid_copy(block, unit, piece):
        return remote(mid.at[unit, :, columns(piece)], mid_peer.at[unit, :, columns(piece)],
                      mid_send.at[block, unit, piece], mid_recv.at[block, unit, piece], other_core)

    def hid_columns(piece, shift):
        return pl.ds(pl.multiple_of(piece * 3 * BLOCK + shift * BLOCK, BLOCK), BLOCK)

    def halo_copy(block, unit, piece, edge):
        start = breadth if edge == 0 else whole
        return remote(hid.at[unit, pl.ds(start, breadth), hid_columns(piece, 1)],
                      halo.at[block, unit, 1 - edge, :, columns(piece)],
                      halo_send.at[block, unit, 1 - edge, piece], halo_recv.at[block, unit, 1 - edge, piece],
                      {"section": section - 2 if edge == 0 else section + 2})

    def outward(unit):
        return remote(own.at[unit, theirs], out.at[units * side + unit],
                      out_send.at[unit], out_recv.at[unit], {"section": twin})

    def fetch(matrix, block, slots, at):
        return pltpu.make_async_copy(matrix.at[block], slots.at[block % 2], weight_sem.at[at, block])

    def each(body):
        lax.fori_loop(0, pieces, lambda piece, carry: (body(piece), carry)[1], 0)

    def dot(left, right):
        return jnp.dot(left, right, preferred_element_type=jnp.float32)

    def spread(unit, start, size, piece, values):
        place = lax.broadcasted_iota(jnp.int32, values.shape, 0) & (breadth - 1)
        rows = pl.ds(start, size)
        before = jnp.where(place == 0, 0.0, pltpu.roll(values, 1, 0))
        after = jnp.where(place == breadth - 1, 0.0, pltpu.roll(values, size - 1, 0))
        hid[unit, rows, hid_columns(piece, 0)] = before.astype(jnp.bfloat16)
        hid[unit, rows, hid_columns(piece, 1)] = values.astype(jnp.bfloat16)
        hid[unit, rows, hid_columns(piece, 2)] = after.astype(jnp.bfloat16)

    def reduce_rows(block, unit, rows, size, start, top, bottom):
        def body(piece):
            cols = columns(piece)
            total = dot(own[unit, rows, :], w_one[block % 2, own_rows, cols])
            total += dot(peer[unit, rows, :], w_one[block % 2, peer_rows, cols])
            values = jnp.maximum(gains[3 * block, cols] * total + biases[3 * block, cols], 0.0)
            spread(unit, start, size, piece, values)

            @pl.when(jnp.logical_and(top, above))
            def _():
                halo_copy(block, unit, piece, 0).start()

            @pl.when(jnp.logical_and(bottom, below))
            def _():
                halo_copy(block, unit, piece, 1).start()

        each(body)

    def reduce_mine(unit):
        lift_first(unit).wait_recv()
        reduce_rows(0, unit, mine, part, pl.multiple_of(breadth + side * part, breadth), side == 0, side == 1)

    def receive(unit):
        swap(unit).wait_recv()
        lift_second(unit).start()

    def reduce_theirs(unit):
        lift_second(unit).wait_recv()
        reduce_rows(0, unit, theirs, part, pl.multiple_of(breadth + (1 - side) * part, breadth), side == 1, side == 0)

    def settle_halo(block, unit):
        def body(piece):
            @pl.when(above)
            def _():
                halo_copy(block, unit, piece, 0).wait_send()

            @pl.when(below)
            def _():
                halo_copy(block, unit, piece, 1).wait_send()

        each(body)

    def reduce_all(block, unit):
        each(lambda piece: cur_copy(block, unit, piece).wait_recv())
        settle_halo(block - 1, unit)
        reduce_rows(block, unit, slice(None), whole, breadth, True, True)

    def convolve(block, unit):
        if block > 0:
            each(lambda piece: mid_copy(block - 1, unit, piece).wait_send())

        def body(piece):
            cols = columns(piece)

            @pl.when(above)
            def _():
                halo_copy(block, unit, piece, 1).wait_recv()
                spread(unit, 0, breadth, piece, halo[block, unit, 0, :, cols].astype(jnp.float32))

            @pl.when(below)
            def _():
                halo_copy(block, unit, piece, 0).wait_recv()
                spread(unit, whole + breadth, breadth, piece, halo[block, unit, 1, :, cols].astype(jnp.float32))

            band = pl.ds(pl.multiple_of(piece * 3 * BLOCK, BLOCK), 3 * BLOCK)
            total = None
            for shift in range(3):
                term = dot(hid[unit, pl.ds(shift * breadth, whole), band],
                           dense[block % 2, pl.ds(shift * 3 * BLOCK, 3 * BLOCK), cols])
                total = term if total is None else total + term
            values = jnp.maximum(gains[3 * block + 1, cols] * total + biases[3 * block + 1, cols], 0.0)
            mid[unit, :, cols] = values.astype(jnp.bfloat16)
            mid_copy(block, unit, piece).start()

        each(body)

    def expand(block, unit):
        each(lambda piece: mid_copy(block, unit, piece).wait_recv())
        if block == 0:
            lift_second(unit).wait_send()
        else:
            each(lambda piece: cur_copy(block, unit, piece).wait_send())

        def body(piece):
            cols = columns(piece)
            total = dot(mid[unit], w_two[block % 2, own_rows, cols])
            total += dot(mid_peer[unit], w_two[block % 2, peer_rows, cols])
            total = gains[3 * block + 2, cols] * total + biases[3 * block + 2, cols]
            values = jnp.maximum(total + own[unit, :, cols].astype(jnp.float32), 0.0)
            own[unit, :, cols] = values.astype(jnp.bfloat16)
            if block < blocks - 1:
                cur_copy(block + 1, unit, piece).start()

        each(body)
        if block == blocks - 1:
            outward(unit).start()
            home(unit).start()

    def home(unit):
        return pltpu.make_async_copy(own.at[unit, mine], out.at[units * side + unit], local_sem.at[unit])

    def stage(unit):
        return pltpu.make_async_copy(planes.at[units * side + unit], own.at[unit, mine], local_sem.at[unit])

    def build(block):
        row = lax.broadcasted_iota(jnp.int32, (BLOCK, BLOCK), 0)
        col = lax.broadcasted_iota(jnp.int32, (BLOCK, BLOCK), 1)
        same = (row // width) == (col // width)

        def tap_body(tap, carry):
            source = pl.ds(pl.multiple_of(tap * width, width), width)
            target = pl.ds(pl.multiple_of(tap * BLOCK, BLOCK), BLOCK)
            for piece in range(pieces):
                cols = pl.ds(piece * BLOCK, BLOCK)
                values = taps[block, source, cols].astype(jnp.float32)
                tiled = jnp.concatenate([values] * (BLOCK // width), axis=0)
                dense[block % 2, target, cols] = jnp.where(same, tiled, 0.0).astype(jnp.bfloat16)
            return carry

        lax.fori_loop(0, 9, tap_body, 0)

    barrier = pltpu.get_barrier_semaphore()
    pl.semaphore_signal(barrier, inc=1, device_id=other_core, device_id_type=MESH)
    pl.semaphore_signal(barrier, inc=1, device_id={"section": twin}, device_id_type=MESH)

    @pl.when(above)
    def _():
        pl.semaphore_signal(barrier, inc=1, device_id={"section": section - 2}, device_id_type=MESH)

    @pl.when(below)
    def _():
        pl.semaphore_signal(barrier, inc=1, device_id={"section": section + 2}, device_id_type=MESH)

    for unit in range(units):
        stage(unit).start()
    group_load = pltpu.make_async_copy(w_group, taps, local_sem.at[units])
    fetch(w_reduce, 0, w_one, 0).start()
    group_load.start()
    fetch(w_expand, 0, w_two, 1).start()
    fetch(w_reduce, 1, w_one, 0).start()
    fetch(w_expand, 1, w_two, 1).start()

    pl.semaphore_wait(barrier, 2 + above.astype(jnp.int32) + below.astype(jnp.int32))

    for unit in range(units):
        swap(unit).start()
    for unit in range(units):
        lift_first(unit).start()
    edge_zeros = jnp.zeros((breadth, hid.shape[2]), hid.dtype)
    for unit in range(units):
        hid[unit, pl.ds(0, breadth), :] = edge_zeros
        hid[unit, pl.ds(whole + breadth, breadth), :] = edge_zeros
    for unit in range(units):
        stage(unit).wait()
    fetch(w_reduce, 0, w_one, 0).wait()
    reduce_mine(0)
    reduce_mine(1)
    group_load.wait()
    build(0)
    build(1)
    fetch(w_expand, 0, w_two, 1).wait()
    fetch(w_reduce, 1, w_one, 0).wait()
    fetch(w_expand, 1, w_two, 1).wait()

    receive(0)
    reduce_theirs(0)
    convolve(0, 0)
    expand(0, 0)
    reduce_all(1, 0)
    receive(1)
    convolve(1, 0)
    reduce_theirs(1)
    fetch(w_reduce, 2, w_one, 0).start()
    expand(1, 0)
    convolve(0, 1)
    build(2)
    fetch(w_reduce, 2, w_one, 0).wait()
    reduce_all(2, 0)
    expand(0, 1)
    fetch(w_expand, 2, w_two, 1).start()
    reduce_all(1, 1)
    convolve(2, 0)
    convolve(1, 1)
    fetch(w_expand, 2, w_two, 1).wait()
    expand(2, 0)
    expand(1, 1)
    reduce_all(2, 1)
    convolve(2, 1)
    expand(2, 1)

    for unit in range(units):
        settle_halo(blocks - 1, unit)
        each(lambda piece: mid_copy(blocks - 1, unit, piece).wait_send())
        swap(unit).wait_send()
        lift_first(unit).wait_send()
        home(unit).wait()
        outward(unit).wait_send()
        outward(unit).wait_recv()


def fused(mesh):
    count = mesh.shape["section"]

    def call(planes, w_reduce, w_group, w_expand, gains, biases):
        tiles, rows, breadth, channels = planes.shape
        blocks, depth, _ = w_reduce.shape
        part, units, pieces = rows * breadth, tiles // 2, channels // BLOCK
        whole, kind = 2 * part, planes.dtype
        dma = pltpu.SemaphoreType.DMA
        scratch = [
            pltpu.VMEM((units, whole, channels), kind),
            pltpu.VMEM((units, whole, channels), kind),
            pltpu.VMEM((units, whole, channels), kind),
            pltpu.VMEM((units, whole, channels), kind),
            pltpu.VMEM((units, whole + 2 * breadth, 3 * channels), kind),
            pltpu.VMEM((blocks, units, 2, breadth, channels), kind),
            pltpu.VMEM((2, depth, channels), kind),
            pltpu.VMEM((2, depth, channels), kind),
            pltpu.VMEM((2, 9 * BLOCK, channels), kind),
            pltpu.VMEM((blocks, 9 * w_group.shape[2], channels), kind),
            dma((units + 1,)), dma((2, blocks)),
            dma((units,)), dma((units,)),
            dma((2, units)), dma((2, units)),
            dma((blocks, units, pieces)), dma((blocks, units, pieces)),
            dma((blocks, units, pieces)), dma((blocks, units, pieces)),
            dma((blocks, units, 2, pieces)), dma((blocks, units, 2, pieces)),
            dma((units,)), dma((units,)),
        ]
        anywhere, inside = pl.BlockSpec(memory_space=pl.ANY), pl.BlockSpec(memory_space=pltpu.VMEM)
        pixels = tiles * part
        flops = 2 * pixels * blocks * channels * (2 * depth + 9 * BLOCK)
        result = pl.pallas_call(
            functools.partial(fused_kernel, count),
            out_shape=jax.ShapeDtypeStruct((tiles, part, channels), kind),
            in_specs=[anywhere] * 4 + [inside] * 2,
            out_specs=anywhere,
            scratch_shapes=scratch,
            compiler_params=pltpu.CompilerParams(
                collective_id=0, has_side_effects=True, vmem_limit_bytes=60 * 1024 * 1024),
            cost_estimate=pl.CostEstimate(flops=flops, bytes_accessed=4 * blocks * depth * channels, transcendentals=0),
        )(
            planes.reshape(tiles, part, channels), w_reduce,
            w_group.reshape(blocks, 9 * w_group.shape[2], channels), w_expand,
            gains.reshape(blocks * 3, channels), biases.reshape(blocks * 3, channels),
        )
        return result.reshape(planes.shape)

    return call


def suits(mesh, planes, w_reduce, w_group):
    tiles, rows, breadth, channels = planes.shape
    return (
        mesh.shape["grp"] == 2 and mesh.shape["section"] % 2 == 0 and tiles == 4
        and channels % BLOCK == 0 and w_reduce.shape[0] == 3
        and breadth % 16 == 0 and breadth & (breadth - 1) == 0
        and w_group.shape[2] % 16 == 0 and BLOCK % w_group.shape[2] == 0
    )


def solution(mesh):
    placed = (
        P(None, "section", None, "grp"),
        P(None, None, "grp"),
        P(None, None, None, "grp"),
        P(None, None, "grp"),
        P(None, None, "grp"),
        P(None, None, "grp"),
    )

    def chosen(planes, w_reduce, w_group, *rest):
        body = fused(mesh) if suits(mesh, planes, w_reduce, w_group) else local
        return body(planes, w_reduce, w_group, *rest)

    return jax.shard_map(
        chosen,
        mesh=mesh,
        in_specs=placed,
        out_specs=P(None, "section", None, "grp"),
        check_vma=False,
    )
```

```python
import functools

import jax
import jax.numpy as jnp
from jax import lax
from jax.experimental import pallas as pl
from jax.experimental.pallas import tpu as pltpu
from jax.sharding import PartitionSpec as P


def extended(cells, sides, width):
    for axis, dim in sides:
        count = lax.axis_size(axis)
        ends = count - 1
        head = lax.slice_in_dim(cells, 0, width, axis=dim)
        tail = lax.slice_in_dim(cells, cells.shape[dim] - width, cells.shape[dim], axis=dim)
        cells = jnp.concatenate(
            [
                lax.ppermute(tail, axis, [(i, (i + 1) % count) for i in range(ends)]),
                cells,
                lax.ppermute(head, axis, [((i + 1) % count, i) for i in range(ends)]),
            ],
            axis=dim,
        )
    return cells


def group_matrix(kernel):
    tap_count, group_width, channels = kernel.shape
    tiled = jnp.tile(kernel, (1, channels // group_width, 1))
    row_group = lax.broadcasted_iota(jnp.int32, (channels, channels), 0) // group_width
    col_group = lax.broadcasted_iota(jnp.int32, (channels, channels), 1) // group_width
    masked = jnp.where((row_group == col_group)[None], tiled, jnp.zeros_like(tiled))
    return masked.reshape(tap_count * channels, channels)


def contract(weight, piece):
    return jnp.dot(piece, weight, preferred_element_type=jnp.float32)


def gather_reduce(flat, weight):
    return contract(weight, lax.all_gather(flat, "grp", axis=1, tiled=True))


def gather_expand(flat, weight):
    return contract(weight, lax.all_gather(flat, "grp", axis=1, tiled=True))


def run_block(planes, w_reduce, kernel, w_expand, gains, biases):
    tiles, rows, breadth, channels = planes.shape
    dense_group = group_matrix(kernel)
    first = gather_reduce(planes.reshape(-1, channels), w_reduce)
    hidden = jnp.maximum(gains[0] * first + biases[0], 0.0).astype(jnp.bfloat16)
    hidden = extended(hidden.reshape(planes.shape), (("section", 1),), 1)
    padded = jnp.pad(hidden, ((0, 0), (0, 0), (1, 1), (0, 0)))
    shifted = [
        padded[:, row_shift : row_shift + rows, col_shift : col_shift + breadth, :]
        for row_shift in range(3)
        for col_shift in range(3)
    ]
    taps = jnp.concatenate(shifted, axis=-1).reshape(tiles * rows * breadth, 9 * channels)
    spatial = jnp.dot(taps, dense_group, preferred_element_type=jnp.float32)
    middle = jnp.maximum(gains[1] * spatial + biases[1], 0.0).astype(jnp.bfloat16)
    second = gather_expand(middle, w_expand)
    stream = planes.reshape(-1, channels).astype(jnp.float32)
    result = jnp.maximum(gains[2] * second + biases[2] + stream, 0.0)
    return result.astype(jnp.bfloat16).reshape(planes.shape)


def local(planes, w_reduce, w_group, w_expand, gains, biases):
    current = planes
    for block in range(w_reduce.shape[0]):
        current = run_block(
            current, w_reduce[block], w_group[block], w_expand[block], gains[block], biases[block]
        )
    return current


BLOCK = 256
MESH = pl.DeviceIdType.MESH


def fused_kernel(
    count, planes, w_reduce, w_group, w_expand, gains, biases, out,
    cur, mid, hid, halo, w_one, w_two, dense, taps,
    local_sem, weight_sem, swap_send, swap_recv, lift_send, lift_recv,
    cur_send, cur_recv, mid_send, mid_recv, halo_send, halo_recv, out_send, out_recv,
):
    blocks, depth, channels = w_reduce.shape[0], w_reduce.shape[1], planes.shape[2]
    part = planes.shape[1]
    whole = 2 * part
    breadth = halo.shape[3]
    pieces = channels // BLOCK
    units = cur.shape[0]
    width = w_group.shape[1] // 9
    section, core = lax.axis_index("section"), lax.axis_index("grp")
    side = lax.rem(section, 2)
    twin = section + 1 - 2 * side
    above, below = section >= 2, section < count - 2
    other_core = {"grp": 1 - core}
    own = pl.ds(pl.multiple_of(core * channels, channels), channels)
    mine = pl.ds(pl.multiple_of(side * part, part), part)
    theirs = pl.ds(pl.multiple_of((1 - side) * part, part), part)

    def remote(src, dst, send, recv, to):
        return pltpu.make_async_remote_copy(
            src_ref=src, dst_ref=dst, send_sem=send, recv_sem=recv, device_id=to, device_id_type=MESH)

    def swap(unit):
        return remote(planes.at[units * (1 - side) + unit], cur.at[unit, mine, own],
                      swap_send.at[unit], swap_recv.at[unit], {"section": twin})

    def lift_first(unit):
        return remote(planes.at[units * side + unit], cur.at[unit, mine, own],
                      lift_send.at[0, unit], lift_recv.at[0, unit], other_core)

    def lift_second(unit):
        return remote(cur.at[unit, theirs, own], cur.at[unit, theirs, own],
                      lift_send.at[1, unit], lift_recv.at[1, unit], other_core)

    def columns(piece):
        return pl.ds(pl.multiple_of(piece * BLOCK, BLOCK), BLOCK)

    def own_columns(piece):
        return pl.ds(pl.multiple_of(core * channels + piece * BLOCK, BLOCK), BLOCK)

    def cur_copy(block, unit, piece):
        return remote(cur.at[unit, :, own_columns(piece)], cur.at[unit, :, own_columns(piece)],
                      cur_send.at[block, unit, piece], cur_recv.at[block, unit, piece], other_core)

    def mid_copy(block, unit, piece):
        return remote(mid.at[unit, :, own_columns(piece)], mid.at[unit, :, own_columns(piece)],
                      mid_send.at[block, unit, piece], mid_recv.at[block, unit, piece], other_core)

    def hid_columns(piece, shift):
        return pl.ds(pl.multiple_of(piece * 3 * BLOCK + shift * BLOCK, BLOCK), BLOCK)

    def halo_copy(block, unit, piece, edge):
        start = breadth if edge == 0 else whole
        return remote(hid.at[unit, pl.ds(start, breadth), hid_columns(piece, 1)],
                      halo.at[block, unit, 1 - edge, :, columns(piece)],
                      halo_send.at[block, unit, 1 - edge, piece], halo_recv.at[block, unit, 1 - edge, piece],
                      {"section": section - 2 if edge == 0 else section + 2})

    def outward(unit, piece):
        return remote(cur.at[unit, theirs, own_columns(piece)], out.at[units * side + unit, :, columns(piece)],
                      out_send.at[unit, piece], out_recv.at[unit, piece], {"section": twin})

    def fetch(matrix, block, slots, at):
        return pltpu.make_async_copy(matrix.at[block], slots.at[block % 2], weight_sem.at[at, block])

    def each(body):
        lax.fori_loop(0, pieces, lambda piece, carry: (body(piece), carry)[1], 0)

    def pairs(work, after):
        def body(at, carry):
            for piece in (2 * at, 2 * at + 1):
                work(piece)
            for piece in (2 * at, 2 * at + 1):
                after(piece)
            return carry

        lax.fori_loop(0, pieces // 2, body, 0)

    def dot(left, right):
        return jnp.dot(left, right, preferred_element_type=jnp.float32)

    def spread(unit, start, size, piece, values):
        place = lax.broadcasted_iota(jnp.int32, values.shape, 0) & (breadth - 1)
        rows = pl.ds(start, size)
        before = jnp.where(place == 0, 0.0, pltpu.roll(values, 1, 0))
        after = jnp.where(place == breadth - 1, 0.0, pltpu.roll(values, size - 1, 0))
        hid[unit, rows, hid_columns(piece, 0)] = before.astype(jnp.bfloat16)
        hid[unit, rows, hid_columns(piece, 1)] = values.astype(jnp.bfloat16)
        hid[unit, rows, hid_columns(piece, 2)] = after.astype(jnp.bfloat16)

    def reduce_rows(block, unit, rows, size, start, top, bottom):
        def body(piece):
            cols = columns(piece)
            total = dot(cur[unit, rows, :], w_one[block % 2, :, cols])
            values = jnp.maximum(gains[block, 0, cols] * total + biases[block, 0, cols], 0.0)
            spread(unit, start, size, piece, values)

        def after(piece):
            @pl.when(jnp.logical_and(top, above))
            def _():
                halo_copy(block, unit, piece, 0).start()

            @pl.when(jnp.logical_and(bottom, below))
            def _():
                halo_copy(block, unit, piece, 1).start()

        pairs(body, after)

    def reduce_mine(unit):
        lift_first(unit).wait_recv()
        reduce_rows(0, unit, mine, part, pl.multiple_of(breadth + side * part, breadth), side == 0, side == 1)

    def receive(unit):
        swap(unit).wait_recv()
        if unit + 1 < units:
            swap(unit + 1).start()
        lift_second(unit).start()

    def reduce_theirs(unit):
        lift_second(unit).wait_recv()
        reduce_rows(0, unit, theirs, part, pl.multiple_of(breadth + (1 - side) * part, breadth), side == 1, side == 0)

    def settle_halo(block, unit):
        def body(piece):
            @pl.when(above)
            def _():
                halo_copy(block, unit, piece, 0).wait_send()

            @pl.when(below)
            def _():
                halo_copy(block, unit, piece, 1).wait_send()

        each(body)

    def reduce_all(block, unit):
        each(lambda piece: cur_copy(block, unit, piece).wait_recv())
        settle_halo(block - 1, unit)
        reduce_rows(block, unit, slice(None), whole, breadth, True, True)

    def convolve(block, unit):
        if block > 0:
            each(lambda piece: mid_copy(block - 1, unit, piece).wait_send())

        def edges(piece):
            cols = columns(piece)

            @pl.when(above)
            def _():
                halo_copy(block, unit, piece, 1).wait_recv()
                spread(unit, 0, breadth, piece, halo[block, unit, 0, :, cols].astype(jnp.float32))

            @pl.when(below)
            def _():
                halo_copy(block, unit, piece, 0).wait_recv()
                spread(unit, whole + breadth, breadth, piece, halo[block, unit, 1, :, cols].astype(jnp.float32))

        def body(piece):
            cols = columns(piece)
            band = pl.ds(pl.multiple_of(piece * 3 * BLOCK, BLOCK), 3 * BLOCK)
            total = None
            for shift in range(3):
                term = dot(hid[unit, pl.ds(shift * breadth, whole), band],
                           dense[block % 2, pl.ds(shift * 3 * BLOCK, 3 * BLOCK), cols])
                total = term if total is None else total + term
            values = jnp.maximum(gains[block, 1, cols] * total + biases[block, 1, cols], 0.0)
            mid[unit, :, own_columns(piece)] = values.astype(jnp.bfloat16)

        each(edges)
        pairs(body, lambda piece: mid_copy(block, unit, piece).start())

    def expand(block, unit):
        each(lambda piece: mid_copy(block, unit, piece).wait_recv())
        if block == 0:
            lift_second(unit).wait_send()
        else:
            each(lambda piece: cur_copy(block, unit, piece).wait_send())

        def body(piece):
            cols = columns(piece)
            total = dot(mid[unit], w_two[block % 2, :, cols])
            total = gains[block, 2, cols] * total + biases[block, 2, cols]
            values = jnp.maximum(total + cur[unit, :, own_columns(piece)].astype(jnp.float32), 0.0)
            cur[unit, :, own_columns(piece)] = values.astype(jnp.bfloat16)

        def after(piece):
            if block < blocks - 1:
                cur_copy(block + 1, unit, piece).start()
            else:
                outward(unit, piece).start()

        pairs(body, after)
        if block == blocks - 1:
            home(unit).start()

    def home(unit):
        return pltpu.make_async_copy(cur.at[unit, mine, own], out.at[units * side + unit], local_sem.at[unit])

    def stage(unit):
        return pltpu.make_async_copy(planes.at[units * side + unit], cur.at[unit, mine, own], local_sem.at[unit])

    def build(block):
        row = lax.broadcasted_iota(jnp.int32, (BLOCK, BLOCK), 0)
        col = lax.broadcasted_iota(jnp.int32, (BLOCK, BLOCK), 1)
        same = (row // width) == (col // width)

        def tap_body(tap, carry):
            source = pl.ds(pl.multiple_of(tap * width, width), width)
            target = pl.ds(pl.multiple_of(tap * BLOCK, BLOCK), BLOCK)
            for piece in range(pieces):
                cols = pl.ds(piece * BLOCK, BLOCK)
                values = taps[block, source, cols].astype(jnp.float32)
                tiled = jnp.concatenate([values] * (BLOCK // width), axis=0)
                dense[block % 2, target, cols] = jnp.where(same, tiled, 0.0).astype(jnp.bfloat16)
            return carry

        lax.fori_loop(0, 9, tap_body, 0)

    barrier = pltpu.get_barrier_semaphore()
    pl.semaphore_signal(barrier, inc=1, device_id=other_core, device_id_type=MESH)
    pl.semaphore_signal(barrier, inc=1, device_id={"section": twin}, device_id_type=MESH)

    @pl.when(above)
    def _():
        pl.semaphore_signal(barrier, inc=1, device_id={"section": section - 2}, device_id_type=MESH)

    @pl.when(below)
    def _():
        pl.semaphore_signal(barrier, inc=1, device_id={"section": section + 2}, device_id_type=MESH)

    for unit in range(units):
        stage(unit).start()
    group_load = pltpu.make_async_copy(w_group, taps, local_sem.at[units])
    fetch(w_reduce, 0, w_one, 0).start()
    group_load.start()
    fetch(w_expand, 0, w_two, 1).start()
    fetch(w_reduce, 1, w_one, 0).start()
    fetch(w_expand, 1, w_two, 1).start()

    pl.semaphore_wait(barrier, 2 + above.astype(jnp.int32) + below.astype(jnp.int32))

    swap(0).start()
    for unit in range(units):
        lift_first(unit).start()
    edge_zeros = jnp.zeros((breadth, hid.shape[2]), hid.dtype)
    for unit in range(units):
        hid[unit, pl.ds(0, breadth), :] = edge_zeros
        hid[unit, pl.ds(whole + breadth, breadth), :] = edge_zeros
    for unit in range(units):
        stage(unit).wait()
    fetch(w_reduce, 0, w_one, 0).wait()
    reduce_mine(0)
    reduce_mine(1)
    group_load.wait()
    build(0)
    build(1)
    fetch(w_expand, 0, w_two, 1).wait()
    fetch(w_reduce, 1, w_one, 0).wait()
    fetch(w_expand, 1, w_two, 1).wait()

    receive(0)
    reduce_theirs(0)
    convolve(0, 0)
    expand(0, 0)
    reduce_all(1, 0)
    receive(1)
    convolve(1, 0)
    reduce_theirs(1)
    fetch(w_reduce, 2, w_one, 0).start()
    expand(1, 0)
    convolve(0, 1)
    build(2)
    fetch(w_reduce, 2, w_one, 0).wait()
    reduce_all(2, 0)
    expand(0, 1)
    fetch(w_expand, 2, w_two, 1).start()
    reduce_all(1, 1)
    convolve(2, 0)
    convolve(1, 1)
    fetch(w_expand, 2, w_two, 1).wait()
    expand(2, 0)
    expand(1, 1)
    reduce_all(2, 1)
    convolve(2, 1)
    expand(2, 1)

    for unit in range(units):
        settle_halo(blocks - 1, unit)
        each(lambda piece: mid_copy(blocks - 1, unit, piece).wait_send())
        swap(unit).wait_send()
        lift_first(unit).wait_send()
        home(unit).wait()
        each(lambda piece: outward(unit, piece).wait_send())
        each(lambda piece: outward(unit, piece).wait_recv())


def fused(mesh):
    count = mesh.shape["section"]

    def call(planes, w_reduce, w_group, w_expand, gains, biases):
        tiles, rows, breadth, channels = planes.shape
        blocks, depth, _ = w_reduce.shape
        part, units, pieces = rows * breadth, tiles // 2, channels // BLOCK
        whole, kind = 2 * part, planes.dtype
        dma = pltpu.SemaphoreType.DMA
        scratch = [
            pltpu.VMEM((units, whole, depth), kind),
            pltpu.VMEM((units, whole, depth), kind),
            pltpu.VMEM((units, whole + 2 * breadth, 3 * channels), kind),
            pltpu.VMEM((blocks, units, 2, breadth, channels), kind),
            pltpu.VMEM((2, depth, channels), kind),
            pltpu.VMEM((2, depth, channels), kind),
            pltpu.VMEM((2, 9 * BLOCK, channels), kind),
            pltpu.VMEM((blocks, 9 * w_group.shape[2], channels), kind),
            dma((units + 1,)), dma((2, blocks)),
            dma((units,)), dma((units,)),
            dma((2, units)), dma((2, units)),
            dma((blocks, units, pieces)), dma((blocks, units, pieces)),
            dma((blocks, units, pieces)), dma((blocks, units, pieces)),
            dma((blocks, units, 2, pieces)), dma((blocks, units, 2, pieces)),
            dma((units, pieces)), dma((units, pieces)),
        ]
        anywhere, inside = pl.BlockSpec(memory_space=pl.ANY), pl.BlockSpec(memory_space=pltpu.VMEM)
        pixels = tiles * part
        flops = 2 * pixels * blocks * channels * (2 * depth + 9 * BLOCK)
        result = pl.pallas_call(
            functools.partial(fused_kernel, count),
            out_shape=jax.ShapeDtypeStruct((tiles, part, channels), kind),
            in_specs=[anywhere] * 4 + [inside] * 2,
            out_specs=anywhere,
            scratch_shapes=scratch,
            compiler_params=pltpu.CompilerParams(
                collective_id=0, has_side_effects=True, vmem_limit_bytes=60 * 1024 * 1024),
            cost_estimate=pl.CostEstimate(flops=flops, bytes_accessed=4 * blocks * depth * channels, transcendentals=0),
        )(
            planes.reshape(tiles, part, channels), w_reduce,
            w_group.reshape(blocks, 9 * w_group.shape[2], channels), w_expand,
            gains, biases,
        )
        return result.reshape(planes.shape)

    return call


def suits(mesh, planes, w_reduce, w_group):
    tiles, rows, breadth, channels = planes.shape
    return (
        mesh.shape["grp"] == 2 and mesh.shape["section"] % 2 == 0 and tiles == 4
        and channels % (2 * BLOCK) == 0 and w_reduce.shape[0] == 3
        and breadth % 16 == 0 and breadth & (breadth - 1) == 0
        and w_group.shape[2] % 16 == 0 and BLOCK % w_group.shape[2] == 0
    )


def solution(mesh):
    placed = (
        P(None, "section", None, "grp"),
        P(None, None, "grp"),
        P(None, None, None, "grp"),
        P(None, None, "grp"),
        P(None, None, "grp"),
        P(None, None, "grp"),
    )

    def chosen(planes, w_reduce, w_group, *rest):
        body = fused(mesh) if suits(mesh, planes, w_reduce, w_group) else local
        return body(planes, w_reduce, w_group, *rest)

    return jax.shard_map(
        chosen,
        mesh=mesh,
        in_specs=placed,
        out_specs=P(None, "section", None, "grp"),
        check_vma=False,
    )
```

```python
import functools

import jax
import jax.numpy as jnp
from jax import lax
from jax.experimental import pallas as pl
from jax.experimental.pallas import tpu as pltpu
from jax.sharding import PartitionSpec as P


def extended(cells, sides, width):
    for axis, dim in sides:
        count = lax.axis_size(axis)
        ends = count - 1
        head = lax.slice_in_dim(cells, 0, width, axis=dim)
        tail = lax.slice_in_dim(cells, cells.shape[dim] - width, cells.shape[dim], axis=dim)
        cells = jnp.concatenate(
            [
                lax.ppermute(tail, axis, [(i, (i + 1) % count) for i in range(ends)]),
                cells,
                lax.ppermute(head, axis, [((i + 1) % count, i) for i in range(ends)]),
            ],
            axis=dim,
        )
    return cells


def group_matrix(kernel):
    tap_count, group_width, channels = kernel.shape
    tiled = jnp.tile(kernel, (1, channels // group_width, 1))
    row_group = lax.broadcasted_iota(jnp.int32, (channels, channels), 0) // group_width
    col_group = lax.broadcasted_iota(jnp.int32, (channels, channels), 1) // group_width
    masked = jnp.where((row_group == col_group)[None], tiled, jnp.zeros_like(tiled))
    return masked.reshape(tap_count * channels, channels)


def contract(weight, piece):
    return jnp.dot(piece, weight, preferred_element_type=jnp.float32)


def gather_reduce(flat, weight):
    return contract(weight, lax.all_gather(flat, "grp", axis=1, tiled=True))


def gather_expand(flat, weight):
    return contract(weight, lax.all_gather(flat, "grp", axis=1, tiled=True))


def run_block(planes, w_reduce, kernel, w_expand, gains, biases):
    tiles, rows, breadth, channels = planes.shape
    dense_group = group_matrix(kernel)
    first = gather_reduce(planes.reshape(-1, channels), w_reduce)
    hidden = jnp.maximum(gains[0] * first + biases[0], 0.0).astype(jnp.bfloat16)
    hidden = extended(hidden.reshape(planes.shape), (("section", 1),), 1)
    padded = jnp.pad(hidden, ((0, 0), (0, 0), (1, 1), (0, 0)))
    shifted = [
        padded[:, row_shift : row_shift + rows, col_shift : col_shift + breadth, :]
        for row_shift in range(3)
        for col_shift in range(3)
    ]
    taps = jnp.concatenate(shifted, axis=-1).reshape(tiles * rows * breadth, 9 * channels)
    spatial = jnp.dot(taps, dense_group, preferred_element_type=jnp.float32)
    middle = jnp.maximum(gains[1] * spatial + biases[1], 0.0).astype(jnp.bfloat16)
    second = gather_expand(middle, w_expand)
    stream = planes.reshape(-1, channels).astype(jnp.float32)
    result = jnp.maximum(gains[2] * second + biases[2] + stream, 0.0)
    return result.astype(jnp.bfloat16).reshape(planes.shape)


def local(planes, w_reduce, w_group, w_expand, gains, biases):
    current = planes
    for block in range(w_reduce.shape[0]):
        current = run_block(
            current, w_reduce[block], w_group[block], w_expand[block], gains[block], biases[block]
        )
    return current


BLOCK = 256
MESH = pl.DeviceIdType.MESH


def fused_kernel(
    count, planes, w_reduce, w_group, w_expand, gains, biases, out,
    cur, mid, hid, halo, w_one, w_two, dense, taps,
    local_sem, weight_sem, swap_send, swap_recv, lift_send, lift_recv,
    cur_send, cur_recv, mid_send, mid_recv, halo_send, halo_recv, out_send, out_recv,
):
    blocks, depth, channels = w_reduce.shape[0], w_reduce.shape[1], planes.shape[2]
    part = planes.shape[1]
    whole = 2 * part
    breadth = halo.shape[3]
    pieces = channels // BLOCK
    units = cur.shape[0]
    width = w_group.shape[1] // 9
    section, core = lax.axis_index("section"), lax.axis_index("grp")
    side = lax.rem(section, 2)
    twin = section + 1 - 2 * side
    above, below = section >= 2, section < count - 2
    other_core = {"grp": 1 - core}
    own = pl.ds(pl.multiple_of(core * channels, channels), channels)
    mine = pl.ds(pl.multiple_of(side * part, part), part)
    theirs = pl.ds(pl.multiple_of((1 - side) * part, part), part)

    def remote(src, dst, send, recv, to):
        return pltpu.make_async_remote_copy(
            src_ref=src, dst_ref=dst, send_sem=send, recv_sem=recv, device_id=to, device_id_type=MESH)

    lines = part // breadth

    def line_rows(half, line):
        return pl.ds(pl.multiple_of(half * part + line * breadth, breadth), breadth)

    def swap(unit, line):
        return remote(planes.at[units * (1 - side) + unit, pl.ds(line * breadth, breadth)],
                      cur.at[unit, line_rows(side, line), own],
                      swap_send.at[unit, line], swap_recv.at[unit, line], {"section": twin})

    def lift_first(unit):
        return remote(planes.at[units * side + unit], cur.at[unit, mine, own],
                      lift_send.at[unit, lines], lift_recv.at[unit, lines], other_core)

    def lift_second(unit, line):
        there = line_rows(1 - side, line)
        return remote(cur.at[unit, there, own], cur.at[unit, there, own],
                      lift_send.at[unit, line], lift_recv.at[unit, line], other_core)

    def columns(piece):
        return pl.ds(pl.multiple_of(piece * BLOCK, BLOCK), BLOCK)

    def own_columns(piece):
        return pl.ds(pl.multiple_of(core * channels + piece * BLOCK, BLOCK), BLOCK)

    def cur_copy(block, unit, piece):
        return remote(cur.at[unit, :, own_columns(piece)], cur.at[unit, :, own_columns(piece)],
                      cur_send.at[block, unit, piece], cur_recv.at[block, unit, piece], other_core)

    def mid_copy(block, unit, piece):
        return remote(mid.at[unit, :, own_columns(piece)], mid.at[unit, :, own_columns(piece)],
                      mid_send.at[block, unit, piece], mid_recv.at[block, unit, piece], other_core)

    def hid_columns(piece, shift):
        return pl.ds(pl.multiple_of(piece * 3 * BLOCK + shift * BLOCK, BLOCK), BLOCK)

    def halo_copy(block, unit, piece, edge):
        start = breadth if edge == 0 else whole
        return remote(hid.at[unit, pl.ds(start, breadth), hid_columns(piece, 1)],
                      halo.at[block, unit, 1 - edge, :, columns(piece)],
                      halo_send.at[block, unit, 1 - edge, piece], halo_recv.at[block, unit, 1 - edge, piece],
                      {"section": section - 2 if edge == 0 else section + 2})

    def outward(unit, piece):
        return remote(cur.at[unit, theirs, own_columns(piece)], out.at[units * side + unit, :, columns(piece)],
                      out_send.at[unit, piece], out_recv.at[unit, piece], {"section": twin})

    def fetch(matrix, block, slots, at):
        return pltpu.make_async_copy(matrix.at[block], slots.at[block % 2], weight_sem.at[at, block])

    def each(body):
        lax.fori_loop(0, pieces, lambda piece, carry: (body(piece), carry)[1], 0)

    def pairs(work, after):
        def body(at, carry):
            for piece in (2 * at, 2 * at + 1):
                work(piece)
            for piece in (2 * at, 2 * at + 1):
                after(piece)
            return carry

        lax.fori_loop(0, pieces // 2, body, 0)

    def dot(left, right):
        return jnp.dot(left, right, preferred_element_type=jnp.float32)

    def spread(unit, start, size, piece, values):
        place = lax.broadcasted_iota(jnp.int32, values.shape, 0) & (breadth - 1)
        rows = pl.ds(start, size)
        before = jnp.where(place == 0, 0.0, pltpu.roll(values, 1, 0))
        after = jnp.where(place == breadth - 1, 0.0, pltpu.roll(values, size - 1, 0))
        hid[unit, rows, hid_columns(piece, 0)] = before.astype(jnp.bfloat16)
        hid[unit, rows, hid_columns(piece, 1)] = values.astype(jnp.bfloat16)
        hid[unit, rows, hid_columns(piece, 2)] = after.astype(jnp.bfloat16)

    def reduce_rows(block, unit, rows, size, start, top, bottom):
        def body(piece):
            cols = columns(piece)
            total = dot(cur[unit, rows, :], w_one[block % 2, :, cols])
            values = jnp.maximum(gains[block, 0, cols] * total + biases[block, 0, cols], 0.0)
            spread(unit, start, size, piece, values)

        def after(piece):
            @pl.when(jnp.logical_and(top, above))
            def _():
                halo_copy(block, unit, piece, 0).start()

            @pl.when(jnp.logical_and(bottom, below))
            def _():
                halo_copy(block, unit, piece, 1).start()

        pairs(body, after)

    def reduce_mine(unit):
        lift_first(unit).wait_recv()
        reduce_rows(0, unit, mine, part, pl.multiple_of(breadth + side * part, breadth), side == 0, side == 1)

    def receive(unit):
        for line in range(lines):
            swap(unit, line).wait_recv()
            lift_second(unit, line).start()

    def reduce_theirs(unit):
        for line in range(lines):
            lift_second(unit, line).wait_recv()
        reduce_rows(0, unit, theirs, part, pl.multiple_of(breadth + (1 - side) * part, breadth), side == 1, side == 0)

    def settle_halo(block, unit):
        def body(piece):
            @pl.when(above)
            def _():
                halo_copy(block, unit, piece, 0).wait_send()

            @pl.when(below)
            def _():
                halo_copy(block, unit, piece, 1).wait_send()

        each(body)

    def reduce_all(block, unit):
        each(lambda piece: cur_copy(block, unit, piece).wait_recv())
        settle_halo(block - 1, unit)
        reduce_rows(block, unit, slice(None), whole, breadth, True, True)

    def convolve(block, unit):
        if block > 0:
            each(lambda piece: mid_copy(block - 1, unit, piece).wait_send())

        def edges(piece):
            cols = columns(piece)

            @pl.when(above)
            def _():
                halo_copy(block, unit, piece, 1).wait_recv()
                spread(unit, 0, breadth, piece, halo[block, unit, 0, :, cols].astype(jnp.float32))

            @pl.when(below)
            def _():
                halo_copy(block, unit, piece, 0).wait_recv()
                spread(unit, whole + breadth, breadth, piece, halo[block, unit, 1, :, cols].astype(jnp.float32))

        def body(piece):
            cols = columns(piece)
            band = pl.ds(pl.multiple_of(piece * 3 * BLOCK, BLOCK), 3 * BLOCK)
            total = None
            for shift in range(3):
                term = dot(hid[unit, pl.ds(shift * breadth, whole), band],
                           dense[block % 2, pl.ds(shift * 3 * BLOCK, 3 * BLOCK), cols])
                total = term if total is None else total + term
            values = jnp.maximum(gains[block, 1, cols] * total + biases[block, 1, cols], 0.0)
            mid[unit, :, own_columns(piece)] = values.astype(jnp.bfloat16)

        each(edges)
        pairs(body, lambda piece: mid_copy(block, unit, piece).start())

    def expand(block, unit):
        each(lambda piece: mid_copy(block, unit, piece).wait_recv())
        if block == 0:
            for line in range(lines):
                lift_second(unit, line).wait_send()
        else:
            each(lambda piece: cur_copy(block, unit, piece).wait_send())

        def body(piece):
            cols = columns(piece)
            total = dot(mid[unit], w_two[block % 2, :, cols])
            total = gains[block, 2, cols] * total + biases[block, 2, cols]
            values = jnp.maximum(total + cur[unit, :, own_columns(piece)].astype(jnp.float32), 0.0)
            cur[unit, :, own_columns(piece)] = values.astype(jnp.bfloat16)

        def after(piece):
            if block < blocks - 1:
                cur_copy(block + 1, unit, piece).start()
            else:
                outward(unit, piece).start()

        pairs(body, after)
        if block == blocks - 1:
            home(unit).start()

    def home(unit):
        return pltpu.make_async_copy(cur.at[unit, mine, own], out.at[units * side + unit], local_sem.at[unit])

    def stage(unit):
        return pltpu.make_async_copy(planes.at[units * side + unit], cur.at[unit, mine, own], local_sem.at[unit])

    def build(block):
        row = lax.broadcasted_iota(jnp.int32, (BLOCK, BLOCK), 0)
        col = lax.broadcasted_iota(jnp.int32, (BLOCK, BLOCK), 1)
        same = (row // width) == (col // width)

        def tap_body(tap, carry):
            source = pl.ds(pl.multiple_of(tap * width, width), width)
            target = pl.ds(pl.multiple_of(tap * BLOCK, BLOCK), BLOCK)
            for piece in range(pieces):
                cols = pl.ds(piece * BLOCK, BLOCK)
                values = taps[block, source, cols].astype(jnp.float32)
                tiled = jnp.concatenate([values] * (BLOCK // width), axis=0)
                dense[block % 2, target, cols] = jnp.where(same, tiled, 0.0).astype(jnp.bfloat16)
            return carry

        lax.fori_loop(0, 9, tap_body, 0)

    barrier = pltpu.get_barrier_semaphore()
    pl.semaphore_signal(barrier, inc=1, device_id=other_core, device_id_type=MESH)
    pl.semaphore_signal(barrier, inc=1, device_id={"section": twin}, device_id_type=MESH)

    @pl.when(above)
    def _():
        pl.semaphore_signal(barrier, inc=1, device_id={"section": section - 2}, device_id_type=MESH)

    @pl.when(below)
    def _():
        pl.semaphore_signal(barrier, inc=1, device_id={"section": section + 2}, device_id_type=MESH)

    for unit in range(units):
        stage(unit).start()
    group_load = pltpu.make_async_copy(w_group, taps, local_sem.at[units])
    fetch(w_reduce, 0, w_one, 0).start()
    group_load.start()
    fetch(w_expand, 0, w_two, 1).start()
    fetch(w_reduce, 1, w_one, 0).start()
    fetch(w_expand, 1, w_two, 1).start()

    pl.semaphore_wait(barrier, 2 + above.astype(jnp.int32) + below.astype(jnp.int32))

    for line in range(lines):
        swap(0, line).start()
    for unit in range(units):
        lift_first(unit).start()
    edge_zeros = jnp.zeros((breadth, hid.shape[2]), hid.dtype)
    for unit in range(units):
        hid[unit, pl.ds(0, breadth), :] = edge_zeros
        hid[unit, pl.ds(whole + breadth, breadth), :] = edge_zeros
    for unit in range(units):
        stage(unit).wait()
    fetch(w_reduce, 0, w_one, 0).wait()
    group_load.wait()
    build(0)
    reduce_mine(0)
    for line in range(lines):
        swap(1, line).start()
    reduce_mine(1)
    build(1)
    fetch(w_expand, 0, w_two, 1).wait()
    fetch(w_reduce, 1, w_one, 0).wait()
    fetch(w_expand, 1, w_two, 1).wait()

    receive(0)
    reduce_theirs(0)
    convolve(0, 0)
    expand(0, 0)
    reduce_all(1, 0)
    receive(1)
    convolve(1, 0)
    reduce_theirs(1)
    fetch(w_reduce, 2, w_one, 0).start()
    expand(1, 0)
    convolve(0, 1)
    build(2)
    fetch(w_reduce, 2, w_one, 0).wait()
    reduce_all(2, 0)
    expand(0, 1)
    fetch(w_expand, 2, w_two, 1).start()
    reduce_all(1, 1)
    convolve(2, 0)
    convolve(1, 1)
    fetch(w_expand, 2, w_two, 1).wait()
    expand(2, 0)
    expand(1, 1)
    reduce_all(2, 1)
    convolve(2, 1)
    expand(2, 1)

    for unit in range(units):
        settle_halo(blocks - 1, unit)
        each(lambda piece: mid_copy(blocks - 1, unit, piece).wait_send())
        for line in range(lines):
            swap(unit, line).wait_send()
        lift_first(unit).wait_send()
        home(unit).wait()
        each(lambda piece: outward(unit, piece).wait_send())
        each(lambda piece: outward(unit, piece).wait_recv())


def fused(mesh):
    count = mesh.shape["section"]

    def call(planes, w_reduce, w_group, w_expand, gains, biases):
        tiles, rows, breadth, channels = planes.shape
        blocks, depth, _ = w_reduce.shape
        part, units, pieces = rows * breadth, tiles // 2, channels // BLOCK
        whole, kind = 2 * part, planes.dtype
        dma = pltpu.SemaphoreType.DMA
        scratch = [
            pltpu.VMEM((units, whole, depth), kind),
            pltpu.VMEM((units, whole, depth), kind),
            pltpu.VMEM((units, whole + 2 * breadth, 3 * channels), kind),
            pltpu.VMEM((blocks, units, 2, breadth, channels), kind),
            pltpu.VMEM((2, depth, channels), kind),
            pltpu.VMEM((2, depth, channels), kind),
            pltpu.VMEM((2, 9 * BLOCK, channels), kind),
            pltpu.VMEM((blocks, 9 * w_group.shape[2], channels), kind),
            dma((units + 1,)), dma((2, blocks)),
            dma((units, rows)), dma((units, rows)),
            dma((units, rows + 1)), dma((units, rows + 1)),
            dma((blocks, units, pieces)), dma((blocks, units, pieces)),
            dma((blocks, units, pieces)), dma((blocks, units, pieces)),
            dma((blocks, units, 2, pieces)), dma((blocks, units, 2, pieces)),
            dma((units, pieces)), dma((units, pieces)),
        ]
        anywhere, inside = pl.BlockSpec(memory_space=pl.ANY), pl.BlockSpec(memory_space=pltpu.VMEM)
        pixels = tiles * part
        flops = 2 * pixels * blocks * channels * (2 * depth + 9 * BLOCK)
        result = pl.pallas_call(
            functools.partial(fused_kernel, count),
            out_shape=jax.ShapeDtypeStruct((tiles, part, channels), kind),
            in_specs=[anywhere] * 4 + [inside] * 2,
            out_specs=anywhere,
            scratch_shapes=scratch,
            compiler_params=pltpu.CompilerParams(
                collective_id=0, has_side_effects=True, vmem_limit_bytes=60 * 1024 * 1024),
            cost_estimate=pl.CostEstimate(flops=flops, bytes_accessed=4 * blocks * depth * channels, transcendentals=0),
        )(
            planes.reshape(tiles, part, channels), w_reduce,
            w_group.reshape(blocks, 9 * w_group.shape[2], channels), w_expand,
            gains, biases,
        )
        return result.reshape(planes.shape)

    return call


def suits(mesh, planes, w_reduce, w_group):
    tiles, rows, breadth, channels = planes.shape
    return (
        mesh.shape["grp"] == 2 and mesh.shape["section"] % 2 == 0 and tiles == 4
        and channels % (2 * BLOCK) == 0 and w_reduce.shape[0] == 3
        and breadth % 16 == 0 and breadth & (breadth - 1) == 0
        and w_group.shape[2] % 16 == 0 and BLOCK % w_group.shape[2] == 0
    )


def solution(mesh):
    placed = (
        P(None, "section", None, "grp"),
        P(None, None, "grp"),
        P(None, None, None, "grp"),
        P(None, None, "grp"),
        P(None, None, "grp"),
        P(None, None, "grp"),
    )

    def chosen(planes, w_reduce, w_group, *rest):
        body = fused(mesh) if suits(mesh, planes, w_reduce, w_group) else local
        return body(planes, w_reduce, w_group, *rest)

    return jax.shard_map(
        chosen,
        mesh=mesh,
        in_specs=placed,
        out_specs=P(None, "section", None, "grp"),
        check_vma=False,
    )
```

```python
import functools

import jax
import jax.numpy as jnp
from jax import lax
from jax.experimental import pallas as pl
from jax.experimental.pallas import tpu as pltpu
from jax.sharding import PartitionSpec as P


def extended(cells, sides, width):
    for axis, dim in sides:
        count = lax.axis_size(axis)
        ends = count - 1
        head = lax.slice_in_dim(cells, 0, width, axis=dim)
        tail = lax.slice_in_dim(cells, cells.shape[dim] - width, cells.shape[dim], axis=dim)
        cells = jnp.concatenate(
            [
                lax.ppermute(tail, axis, [(i, (i + 1) % count) for i in range(ends)]),
                cells,
                lax.ppermute(head, axis, [((i + 1) % count, i) for i in range(ends)]),
            ],
            axis=dim,
        )
    return cells


def group_matrix(kernel):
    tap_count, group_width, channels = kernel.shape
    tiled = jnp.tile(kernel, (1, channels // group_width, 1))
    row_group = lax.broadcasted_iota(jnp.int32, (channels, channels), 0) // group_width
    col_group = lax.broadcasted_iota(jnp.int32, (channels, channels), 1) // group_width
    masked = jnp.where((row_group == col_group)[None], tiled, jnp.zeros_like(tiled))
    return masked.reshape(tap_count * channels, channels)


def contract(weight, piece):
    return jnp.dot(piece, weight, preferred_element_type=jnp.float32)


def gather_reduce(flat, weight):
    return contract(weight, lax.all_gather(flat, "grp", axis=1, tiled=True))


def gather_expand(flat, weight):
    return contract(weight, lax.all_gather(flat, "grp", axis=1, tiled=True))


def run_block(planes, w_reduce, kernel, w_expand, gains, biases):
    tiles, rows, breadth, channels = planes.shape
    dense_group = group_matrix(kernel)
    first = gather_reduce(planes.reshape(-1, channels), w_reduce)
    hidden = jnp.maximum(gains[0] * first + biases[0], 0.0).astype(jnp.bfloat16)
    hidden = extended(hidden.reshape(planes.shape), (("section", 1),), 1)
    padded = jnp.pad(hidden, ((0, 0), (0, 0), (1, 1), (0, 0)))
    shifted = [
        padded[:, row_shift : row_shift + rows, col_shift : col_shift + breadth, :]
        for row_shift in range(3)
        for col_shift in range(3)
    ]
    taps = jnp.concatenate(shifted, axis=-1).reshape(tiles * rows * breadth, 9 * channels)
    spatial = jnp.dot(taps, dense_group, preferred_element_type=jnp.float32)
    middle = jnp.maximum(gains[1] * spatial + biases[1], 0.0).astype(jnp.bfloat16)
    second = gather_expand(middle, w_expand)
    stream = planes.reshape(-1, channels).astype(jnp.float32)
    result = jnp.maximum(gains[2] * second + biases[2] + stream, 0.0)
    return result.astype(jnp.bfloat16).reshape(planes.shape)


def local(planes, w_reduce, w_group, w_expand, gains, biases):
    current = planes
    for block in range(w_reduce.shape[0]):
        current = run_block(
            current, w_reduce[block], w_group[block], w_expand[block], gains[block], biases[block]
        )
    return current


BLOCK = 256
MESH = pl.DeviceIdType.MESH


def fused_kernel(
    count, planes, w_reduce, w_group, w_expand, gains, biases, out,
    cur, mid, hid, halo, w_one, w_two, dense, taps,
    local_sem, weight_sem, swap_send, swap_recv, lift_send, lift_recv,
    cur_send, cur_recv, mid_send, mid_recv, halo_send, halo_recv, out_send, out_recv,
):
    blocks, depth, channels = w_reduce.shape[0], w_reduce.shape[1], planes.shape[2]
    part = planes.shape[1]
    whole = 2 * part
    breadth = halo.shape[3]
    pieces = channels // BLOCK
    units = cur.shape[0]
    width = w_group.shape[1] // 9
    section, core = lax.axis_index("section"), lax.axis_index("grp")
    side = lax.rem(section, 2)
    twin = section + 1 - 2 * side
    above, below = section >= 2, section < count - 2
    other_core = {"grp": 1 - core}
    own = pl.ds(pl.multiple_of(core * channels, channels), channels)
    mine = pl.ds(pl.multiple_of(side * part, part), part)
    theirs = pl.ds(pl.multiple_of((1 - side) * part, part), part)

    def remote(src, dst, send, recv, to):
        return pltpu.make_async_remote_copy(
            src_ref=src, dst_ref=dst, send_sem=send, recv_sem=recv, device_id=to, device_id_type=MESH)

    lines = part // breadth

    def line_rows(half, line):
        return pl.ds(pl.multiple_of(half * part + line * breadth, breadth), breadth)

    def swap(unit, line):
        return remote(planes.at[units * (1 - side) + unit, pl.ds(line * breadth, breadth)],
                      cur.at[unit, line_rows(side, line), own],
                      swap_send.at[unit, line], swap_recv.at[unit, line], {"section": twin})

    def lift_first(unit):
        return remote(planes.at[units * side + unit], cur.at[unit, mine, own],
                      lift_send.at[unit, lines], lift_recv.at[unit, lines], other_core)

    def lift_second(unit, line):
        there = line_rows(1 - side, line)
        return remote(cur.at[unit, there, own], cur.at[unit, there, own],
                      lift_send.at[unit, line], lift_recv.at[unit, line], other_core)

    def columns(piece):
        return pl.ds(pl.multiple_of(piece * BLOCK, BLOCK), BLOCK)

    def own_columns(piece):
        return pl.ds(pl.multiple_of(core * channels + piece * BLOCK, BLOCK), BLOCK)

    def cur_copy(block, unit, piece):
        return remote(cur.at[unit, :, own_columns(piece)], cur.at[unit, :, own_columns(piece)],
                      cur_send.at[block, unit, piece], cur_recv.at[block, unit, piece], other_core)

    def mid_copy(block, unit, piece):
        return remote(mid.at[unit, :, own_columns(piece)], mid.at[unit, :, own_columns(piece)],
                      mid_send.at[block, unit, piece], mid_recv.at[block, unit, piece], other_core)

    def hid_columns(piece, shift):
        return pl.ds(pl.multiple_of(piece * 3 * BLOCK + shift * BLOCK, BLOCK), BLOCK)

    def halo_copy(block, unit, piece, edge):
        start = breadth if edge == 0 else whole
        return remote(hid.at[unit, pl.ds(start, breadth), hid_columns(piece, 1)],
                      halo.at[block, unit, 1 - edge, :, columns(piece)],
                      halo_send.at[block, unit, 1 - edge, piece], halo_recv.at[block, unit, 1 - edge, piece],
                      {"section": section - 2 if edge == 0 else section + 2})

    def outward(unit, piece):
        return remote(cur.at[unit, theirs, own_columns(piece)], out.at[units * side + unit, :, columns(piece)],
                      out_send.at[unit, piece], out_recv.at[unit, piece], {"section": twin})

    def fetch(matrix, block, slots, at):
        return pltpu.make_async_copy(matrix.at[block], slots.at[block % 2], weight_sem.at[at, block])

    def each(body):
        lax.fori_loop(0, pieces, lambda piece, carry: (body(piece), carry)[1], 0)

    def steps(work, after):
        def body(at, carry):
            work(at)
            after(at)
            return carry

        lax.fori_loop(0, pieces, body, 0)

    def dot(left, right):
        return jnp.dot(left, right, preferred_element_type=jnp.float32)

    def spread(unit, start, size, piece, values):
        place = lax.broadcasted_iota(jnp.int32, values.shape, 0) & (breadth - 1)
        rows = pl.ds(start, size)
        before = jnp.where(place == 0, 0.0, pltpu.roll(values, 1, 0))
        after = jnp.where(place == breadth - 1, 0.0, pltpu.roll(values, size - 1, 0))
        hid[unit, rows, hid_columns(piece, 0)] = before.astype(jnp.bfloat16)
        hid[unit, rows, hid_columns(piece, 1)] = values.astype(jnp.bfloat16)
        hid[unit, rows, hid_columns(piece, 2)] = after.astype(jnp.bfloat16)

    def reduce_rows(block, unit, rows, size, start, top, bottom):
        def body(piece):
            cols = columns(piece)
            total = dot(cur[unit, rows, :channels], w_one[block % 2, :channels, cols])
            total += dot(cur[unit, rows, channels:], w_one[block % 2, channels:, cols])
            values = jnp.maximum(gains[block, 0, cols] * total + biases[block, 0, cols], 0.0)
            spread(unit, start, size, piece, values)

        def after(piece):
            @pl.when(jnp.logical_and(top, above))
            def _():
                halo_copy(block, unit, piece, 0).start()

            @pl.when(jnp.logical_and(bottom, below))
            def _():
                halo_copy(block, unit, piece, 1).start()

        steps(body, after)

    def reduce_mine(unit):
        lift_first(unit).wait_recv()
        reduce_rows(0, unit, mine, part, pl.multiple_of(breadth + side * part, breadth), side == 0, side == 1)

    def receive(unit):
        for line in range(lines):
            swap(unit, line).wait_recv()
            lift_second(unit, line).start()

    def reduce_theirs(unit):
        for line in range(lines):
            lift_second(unit, line).wait_recv()
        reduce_rows(0, unit, theirs, part, pl.multiple_of(breadth + (1 - side) * part, breadth), side == 1, side == 0)

    def settle_halo(block, unit):
        def body(piece):
            @pl.when(above)
            def _():
                halo_copy(block, unit, piece, 0).wait_send()

            @pl.when(below)
            def _():
                halo_copy(block, unit, piece, 1).wait_send()

        each(body)

    def reduce_all(block, unit):
        each(lambda piece: cur_copy(block, unit, piece).wait_recv())
        settle_halo(block - 1, unit)
        reduce_rows(block, unit, slice(None), whole, breadth, True, True)

    def convolve(block, unit):
        if block > 0:
            each(lambda piece: mid_copy(block - 1, unit, piece).wait_send())

        def edges(piece):
            cols = columns(piece)

            @pl.when(above)
            def _():
                halo_copy(block, unit, piece, 1).wait_recv()
                spread(unit, 0, breadth, piece, halo[block, unit, 0, :, cols].astype(jnp.float32))

            @pl.when(below)
            def _():
                halo_copy(block, unit, piece, 0).wait_recv()
                spread(unit, whole + breadth, breadth, piece, halo[block, unit, 1, :, cols].astype(jnp.float32))

        def body(piece):
            cols = columns(piece)
            band = pl.ds(pl.multiple_of(piece * 3 * BLOCK, BLOCK), 3 * BLOCK)
            total = None
            for shift in range(3):
                term = dot(hid[unit, pl.ds(shift * breadth, whole), band],
                           dense[block % 2, pl.ds(shift * 3 * BLOCK, 3 * BLOCK), cols])
                total = term if total is None else total + term
            values = jnp.maximum(gains[block, 1, cols] * total + biases[block, 1, cols], 0.0)
            mid[unit, :, own_columns(piece)] = values.astype(jnp.bfloat16)

        each(edges)
        steps(body, lambda piece: mid_copy(block, unit, piece).start())

    def expand(block, unit):
        each(lambda piece: mid_copy(block, unit, piece).wait_recv())
        if block == 0:
            for line in range(lines):
                lift_second(unit, line).wait_send()
        else:
            each(lambda piece: cur_copy(block, unit, piece).wait_send())

        def body(piece):
            cols = columns(piece)
            total = dot(mid[unit, :, :channels], w_two[block % 2, :channels, cols])
            total += dot(mid[unit, :, channels:], w_two[block % 2, channels:, cols])
            total = gains[block, 2, cols] * total + biases[block, 2, cols]
            values = jnp.maximum(total + cur[unit, :, own_columns(piece)].astype(jnp.float32), 0.0)
            cur[unit, :, own_columns(piece)] = values.astype(jnp.bfloat16)

        def after(piece):
            if block < blocks - 1:
                cur_copy(block + 1, unit, piece).start()
            else:
                outward(unit, piece).start()

        steps(body, after)
        if block == blocks - 1:
            home(unit).start()

    def home(unit):
        return pltpu.make_async_copy(cur.at[unit, mine, own], out.at[units * side + unit], local_sem.at[unit])

    def stage(unit):
        return pltpu.make_async_copy(planes.at[units * side + unit], cur.at[unit, mine, own], local_sem.at[unit])

    def build(block):
        row = lax.broadcasted_iota(jnp.int32, (BLOCK, BLOCK), 0)
        col = lax.broadcasted_iota(jnp.int32, (BLOCK, BLOCK), 1)
        same = (row // width) == (col // width)

        def tap_body(tap, carry):
            source = pl.ds(pl.multiple_of(tap * width, width), width)
            target = pl.ds(pl.multiple_of(tap * BLOCK, BLOCK), BLOCK)
            for piece in range(pieces):
                cols = pl.ds(piece * BLOCK, BLOCK)
                values = taps[block, source, cols].astype(jnp.float32)
                tiled = jnp.concatenate([values] * (BLOCK // width), axis=0)
                dense[block % 2, target, cols] = jnp.where(same, tiled, 0.0).astype(jnp.bfloat16)
            return carry

        lax.fori_loop(0, 9, tap_body, 0)

    barrier = pltpu.get_barrier_semaphore()
    pl.semaphore_signal(barrier, inc=1, device_id=other_core, device_id_type=MESH)
    pl.semaphore_signal(barrier, inc=1, device_id={"section": twin}, device_id_type=MESH)

    @pl.when(above)
    def _():
        pl.semaphore_signal(barrier, inc=1, device_id={"section": section - 2}, device_id_type=MESH)

    @pl.when(below)
    def _():
        pl.semaphore_signal(barrier, inc=1, device_id={"section": section + 2}, device_id_type=MESH)

    for unit in range(units):
        stage(unit).start()
    group_load = pltpu.make_async_copy(w_group, taps, local_sem.at[units])
    fetch(w_reduce, 0, w_one, 0).start()
    group_load.start()
    fetch(w_expand, 0, w_two, 1).start()
    fetch(w_reduce, 1, w_one, 0).start()
    fetch(w_expand, 1, w_two, 1).start()

    pl.semaphore_wait(barrier, 2 + above.astype(jnp.int32) + below.astype(jnp.int32))

    for line in range(lines):
        swap(0, line).start()
    for unit in range(units):
        lift_first(unit).start()
    edge_zeros = jnp.zeros((breadth, hid.shape[2]), hid.dtype)
    for unit in range(units):
        hid[unit, pl.ds(0, breadth), :] = edge_zeros
        hid[unit, pl.ds(whole + breadth, breadth), :] = edge_zeros
    for unit in range(units):
        stage(unit).wait()
    fetch(w_reduce, 0, w_one, 0).wait()
    group_load.wait()
    build(0)
    reduce_mine(0)
    for line in range(lines):
        swap(1, line).start()
    reduce_mine(1)
    build(1)
    fetch(w_expand, 0, w_two, 1).wait()
    fetch(w_reduce, 1, w_one, 0).wait()
    fetch(w_expand, 1, w_two, 1).wait()

    receive(0)
    reduce_theirs(0)
    convolve(0, 0)
    expand(0, 0)
    reduce_all(1, 0)
    receive(1)
    convolve(1, 0)
    reduce_theirs(1)
    fetch(w_reduce, 2, w_one, 0).start()
    expand(1, 0)
    convolve(0, 1)
    build(2)
    fetch(w_reduce, 2, w_one, 0).wait()
    reduce_all(2, 0)
    expand(0, 1)
    fetch(w_expand, 2, w_two, 1).start()
    reduce_all(1, 1)
    convolve(2, 0)
    convolve(1, 1)
    fetch(w_expand, 2, w_two, 1).wait()
    expand(2, 0)
    expand(1, 1)
    reduce_all(2, 1)
    convolve(2, 1)
    expand(2, 1)

    for unit in range(units):
        settle_halo(blocks - 1, unit)
        each(lambda piece: mid_copy(blocks - 1, unit, piece).wait_send())
        for line in range(lines):
            swap(unit, line).wait_send()
        lift_first(unit).wait_send()
        home(unit).wait()
        each(lambda piece: outward(unit, piece).wait_send())
        each(lambda piece: outward(unit, piece).wait_recv())


def fused(mesh):
    count = mesh.shape["section"]

    def call(planes, w_reduce, w_group, w_expand, gains, biases):
        tiles, rows, breadth, channels = planes.shape
        blocks, depth, _ = w_reduce.shape
        part, units, pieces = rows * breadth, tiles // 2, channels // BLOCK
        whole, kind = 2 * part, planes.dtype
        dma = pltpu.SemaphoreType.DMA
        scratch = [
            pltpu.VMEM((units, whole, depth), kind),
            pltpu.VMEM((units, whole, depth), kind),
            pltpu.VMEM((units, whole + 2 * breadth, 3 * channels), kind),
            pltpu.VMEM((blocks, units, 2, breadth, channels), kind),
            pltpu.VMEM((2, depth, channels), kind),
            pltpu.VMEM((2, depth, channels), kind),
            pltpu.VMEM((2, 9 * BLOCK, channels), kind),
            pltpu.VMEM((blocks, 9 * w_group.shape[2], channels), kind),
            dma((units + 1,)), dma((2, blocks)),
            dma((units, rows)), dma((units, rows)),
            dma((units, rows + 1)), dma((units, rows + 1)),
            dma((blocks, units, pieces)), dma((blocks, units, pieces)),
            dma((blocks, units, pieces)), dma((blocks, units, pieces)),
            dma((blocks, units, 2, pieces)), dma((blocks, units, 2, pieces)),
            dma((units, pieces)), dma((units, pieces)),
        ]
        anywhere, inside = pl.BlockSpec(memory_space=pl.ANY), pl.BlockSpec(memory_space=pltpu.VMEM)
        pixels = tiles * part
        flops = 2 * pixels * blocks * channels * (2 * depth + 9 * BLOCK)
        result = pl.pallas_call(
            functools.partial(fused_kernel, count),
            out_shape=jax.ShapeDtypeStruct((tiles, part, channels), kind),
            in_specs=[anywhere] * 4 + [inside] * 2,
            out_specs=anywhere,
            scratch_shapes=scratch,
            compiler_params=pltpu.CompilerParams(
                collective_id=0, has_side_effects=True, vmem_limit_bytes=60 * 1024 * 1024),
            cost_estimate=pl.CostEstimate(flops=flops, bytes_accessed=4 * blocks * depth * channels, transcendentals=0),
        )(
            planes.reshape(tiles, part, channels), w_reduce,
            w_group.reshape(blocks, 9 * w_group.shape[2], channels), w_expand,
            gains, biases,
        )
        return result.reshape(planes.shape)

    return call


def suits(mesh, planes, w_reduce, w_group):
    tiles, rows, breadth, channels = planes.shape
    return (
        mesh.shape["grp"] == 2 and mesh.shape["section"] % 2 == 0 and tiles == 4
        and channels % (2 * BLOCK) == 0 and w_reduce.shape[0] == 3
        and breadth % 16 == 0 and breadth & (breadth - 1) == 0
        and w_group.shape[2] % 16 == 0 and BLOCK % w_group.shape[2] == 0
    )


def solution(mesh):
    placed = (
        P(None, "section", None, "grp"),
        P(None, None, "grp"),
        P(None, None, None, "grp"),
        P(None, None, "grp"),
        P(None, None, "grp"),
        P(None, None, "grp"),
    )

    def chosen(planes, w_reduce, w_group, *rest):
        body = fused(mesh) if suits(mesh, planes, w_reduce, w_group) else local
        return body(planes, w_reduce, w_group, *rest)

    return jax.shard_map(
        chosen,
        mesh=mesh,
        in_specs=placed,
        out_specs=P(None, "section", None, "grp"),
        check_vma=False,
    )
```
